32 devices in a mesh: freq: 8 (over y, x, core), stn: 4 (over z).
Axes of the slice: x: 2, y: 2, z: 4, core: 2. Of those that a mesh axis runs over, the one named last changes fastest.
Arguments:
- voltages: bfloat16 [512, 16, 4096], P('stn', 'freq'), may hold values from -6 to 6
- filter_taps: float32 [16, 4096], replicated, may hold values from -1.5 to 1.5
- station_flags: int32 [256, 16], replicated, may hold values from 0 to 1, as said below
Outputs:
- visibilities: float32 [256, 512, 512], P('freq', 'stn')
The draws below stay inside these ranges and needn't reach their ends.
Inputs may be any that keep to these rules, and one draw needn't show every extreme that they name: `station_flags`: 1 keeps a station's data in that spectrum, 0 flags it.
All inputs are finite; a program needn't handle non-finite values.
Results may differ from the reference program's by a relative error of at most 0.0039.
Values may be sent and summed in bfloat16 or wider, within the bound.
A program may use at most 192 MiB of HBM per device.

```python
import math
import jax
import jax.numpy as jnp
from jax import lax

C = 4096
TAPS = 16
AVG = 16
STATIONS = 256
SIGNALS = 512
SPECTRA = 16
GROUPS = 256
N_STN = 4


def draw_station_flags(key, part):
    key = jax.random.fold_in(key, 5)
    first_key, second_key = jax.random.split(key)
    levels = jax.random.randint(first_key, (STATIONS, 1), 0, 9)
    rolls = jax.random.randint(second_key, (STATIONS, SPECTRA), 0, 8)
    return (rolls < levels).astype(jnp.int32)


def block_scale(key, shape, cuts, low, high):
    level, own = 1.0, jax.random.fold_in(key, 6)
    for position, shards_of in cuts:
        heights = jnp.exp(jax.random.uniform(jax.random.fold_in(own, position), (shards_of,), jnp.float32, low / len(cuts), high / len(cuts)))
        level = level * jnp.repeat(heights, shape[position] // shards_of).reshape([-1 if axis == position else 1 for axis in range(len(shape))])
    return level


def noise(key, shape, scale, most, pieces=(), kind=jnp.bfloat16):
    array = jax.random.normal(key, shape, jnp.float32) * scale
    if len(pieces) > 0:
        array = block_scale(key, shape, pieces, -0.22, 0.18) * array
    return jnp.clip(array, min=-most, max=most).astype(kind)


def setup_inputs(seed: int = 0) -> dict:
    key_list = jax.random.split(jax.random.key(seed), 4)
    voltages = noise(key_list[0], (SIGNALS, SPECTRA, C), 1.0, 6.0, ((0, 4), (1, 8)))
    filter_taps = noise(key_list[1], (TAPS, C), TAPS ** -0.5, 1.5, (), jnp.float32)
    station_flags = draw_station_flags(jax.random.fold_in(key_list[3], 71), 0)
    return dict(voltages=voltages, filter_taps=filter_taps, station_flags=station_flags)


def channelize(signal_block, filter_taps):
    padded = jnp.pad(signal_block.astype(jnp.float32), ((0, 0), (TAPS - 1, 0), (0, 0)))
    window = jnp.zeros(signal_block.shape, jnp.float32)
    for tap_index in range(TAPS):
        offset = TAPS - 1 - tap_index
        window = window + filter_taps[tap_index][None, None, :] * padded[:, offset:offset + SPECTRA, :]
    positions = jnp.arange(C).astype(jnp.float32)
    pre_angle = math.pi * positions / (2 * C)
    twisted = window * jnp.cos(pre_angle) - 1j * (window * jnp.sin(pre_angle))
    spectrum = jnp.fft.fft(twisted, axis=-1)
    post_angle = math.pi * (2 * positions + 1) / (4 * C)
    result = math.sqrt(2.0 / C) * (jnp.real(spectrum) * jnp.cos(post_angle) + jnp.imag(spectrum) * jnp.sin(post_angle))
    return result.astype(jnp.bfloat16)

def reference(voltages, filter_taps, station_flags):
    per_block = SIGNALS // N_STN
    grouped = voltages.reshape(N_STN, per_block, SPECTRA, C)
    channelized = lax.map(lambda part_block: channelize(part_block, filter_taps), grouped)
    channelized = channelized.reshape(SIGNALS, SPECTRA, C)
    keep = jnp.repeat(station_flags, 2, axis=0).astype(jnp.float32)
    kept = channelized * keep[:, :, None].astype(jnp.bfloat16)
    counts = jnp.dot(keep, keep.T, precision=lax.Precision.HIGHEST)
    arranged = kept.reshape(SIGNALS, SPECTRA, GROUPS, AVG).transpose(2, 0, 1, 3).reshape(GROUPS, SIGNALS, SPECTRA * AVG)
    sums = lax.map(lambda rows_group: jnp.dot(rows_group, rows_group.T, preferred_element_type=jnp.float32), arranged)
    return sums / (AVG * jnp.maximum(counts, 1.0))[None]
```

```python
import functools
import math

import jax
import jax.numpy as jnp
import ml_dtypes
import numpy as np
from jax import lax
from jax.experimental import pallas as pl
from jax.experimental.pallas import tpu as pltpu
from jax.sharding import PartitionSpec as P

MESH = pl.DeviceIdType.MESH
LANES = 128
ROWS = 16

AVG = 16


def from_behind(block, axis, distance):
    devices = range(lax.axis_size(axis))
    route = [(i - distance, i) for i in devices if i - distance in devices]
    return lax.ppermute(block, axis, route)


def dct_four(rows):
    highest = lax.Precision.HIGHEST
    count_rows, channels = rows.shape
    inner_len = 128
    outer_len = channels // inner_len
    positions = jnp.arange(channels).astype(jnp.float32)
    theta = math.pi * positions / (2 * channels)
    real_part = (rows * jnp.cos(theta)).reshape(count_rows, outer_len, inner_len)
    imag_part = (-rows * jnp.sin(theta)).reshape(count_rows, outer_len, inner_len)
    outer_idx = jnp.arange(outer_len, dtype=jnp.int32)
    outer_phase = (
        2
        * math.pi
        * (outer_idx[:, None] * outer_idx[None, :] % outer_len).astype(jnp.float32)
        / outer_len
    )
    outer_cos = jnp.cos(outer_phase)
    outer_sin = jnp.sin(outer_phase)
    section_real = jnp.einsum("pab,ak->pkb", real_part, outer_cos, precision=highest) + jnp.einsum(
        "pab,ak->pkb", imag_part, outer_sin, precision=highest
    )
    section_imag = jnp.einsum("pab,ak->pkb", imag_part, outer_cos, precision=highest) - jnp.einsum(
        "pab,ak->pkb", real_part, outer_sin, precision=highest
    )
    inner_idx = jnp.arange(inner_len, dtype=jnp.int32)
    twist_phase = (
        2 * math.pi * (outer_idx[:, None] * inner_idx[None, :]).astype(jnp.float32) / channels
    )
    twist_cos = jnp.cos(twist_phase)
    twist_sin = jnp.sin(twist_phase)
    twist_real = section_real * twist_cos + section_imag * twist_sin
    twist_imag = section_imag * twist_cos - section_real * twist_sin
    inner_phase = (
        2
        * math.pi
        * (inner_idx[:, None] * inner_idx[None, :] % inner_len).astype(jnp.float32)
        / inner_len
    )
    inner_cos = jnp.cos(inner_phase)
    inner_sin = jnp.sin(inner_phase)
    final_real = jnp.einsum("pkb,bq->pqk", twist_real, inner_cos, precision=highest) + jnp.einsum(
        "pkb,bq->pqk", twist_imag, inner_sin, precision=highest
    )
    final_imag = jnp.einsum("pkb,bq->pqk", twist_imag, inner_cos, precision=highest) - jnp.einsum(
        "pkb,bq->pqk", twist_real, inner_sin, precision=highest
    )
    final_real = final_real.reshape(count_rows, channels)
    final_imag = final_imag.reshape(count_rows, channels)
    post_angle = math.pi * (2 * positions + 1) / (4 * channels)
    return math.sqrt(2.0 / channels) * (
        final_real * jnp.cos(post_angle) + final_imag * jnp.sin(post_angle)
    )


def make_tile(mine, theirs):
    return jnp.einsum("gax,gbx->gab", mine, theirs, preferred_element_type=jnp.float32)


def plain_body(voltages, filter_taps, station_flags):
    sig_dev, spec_dev, channels = voltages.shape
    tap_count = filter_taps.shape[0]
    history_len = tap_count - 1
    reach_count = -(-history_len // spec_dev)
    earlier = []
    for distance in range(1, reach_count + 1):
        needed = min(spec_dev, history_len - (distance - 1) * spec_dev)
        earlier.append(from_behind(voltages[:, spec_dev - needed :, :], "freq", distance))
    frames = jnp.concatenate(earlier[::-1] + [voltages], axis=1)
    window = jnp.zeros((sig_dev, spec_dev, channels), jnp.float32)
    for tap_index in range(tap_count):
        offset = history_len - tap_index
        window = window + filter_taps[tap_index][None, None, :] * frames[
            :, offset : offset + spec_dev, :
        ].astype(jnp.float32)
    channelized = dct_four(window.reshape(sig_dev * spec_dev, channels)).astype(jnp.bfloat16)
    groups_all = channels // AVG
    arranged = (
        channelized.reshape(sig_dev, spec_dev, groups_all, AVG)
        .transpose(2, 0, 1, 3)
        .reshape(groups_all, sig_dev, spec_dev * AVG)
    )
    turned = lax.all_to_all(arranged, "freq", split_axis=0, concat_axis=2, tiled=True)
    signal_flags = jnp.repeat(station_flags, 2, axis=0).astype(jnp.float32)
    position = lax.axis_index("stn")
    own_flags = lax.dynamic_slice_in_dim(signal_flags, position * sig_dev, sig_dev, 0)
    keep = jnp.repeat(own_flags, AVG, axis=1).astype(jnp.bfloat16)
    local = turned * keep[None]
    counts = jnp.dot(own_flags, signal_flags.T, precision=lax.Precision.HIGHEST)
    denominator = AVG * jnp.maximum(counts, 1.0)
    totals = make_tile(local, lax.all_gather(local, "stn", axis=1, tiled=True))
    return totals / denominator[None]


def dft_tables(channels):
    sections = channels // AVG
    k_low = np.arange(AVG)[:, None]
    j_low = np.arange(sections)[None, :]
    turn = 2 * np.pi / channels * (j_low * (k_low + 0.25) + k_low / 4 + 0.125)
    scale = math.sqrt(2.0 / channels)
    twist_cos = (scale * np.cos(turn)).astype(np.float32)
    twist_sin = (scale * np.sin(turn)).astype(np.float32)
    angle = 2 * np.pi / sections * (np.arange(sections)[:, None] * (j_low + 0.25))
    full = np.concatenate([np.cos(angle), np.sin(angle)], axis=1)
    high = full.astype(ml_dtypes.bfloat16)
    low = (full - high.astype(np.float64)).astype(ml_dtypes.bfloat16)
    return twist_cos, twist_sin, high, low


def short_dft(pieces):
    quarter = {}
    for b in range(4):
        for c in range(4):
            real = pieces[b]
            imag = None
            for a in range(1, 4):
                phase = 2 * math.pi * a * (c + 0.25) / 4
                part = pieces[4 * a + b]
                real = real + part * math.cos(phase)
                term = part * -math.sin(phase)
                imag = term if imag is None else imag + term
            if b > 0:
                phase = 2 * math.pi * b * (c + 0.25) / 16
                co, si = math.cos(phase), math.sin(phase)
                real, imag = real * co + imag * si, imag * co - real * si
            quarter[b, c] = (real, imag)
    out = [None] * 16
    for c in range(4):
        (r0, i0), (r1, i1), (r2, i2), (r3, i3) = (quarter[b, c] for b in range(4))
        er, ei, fr, fi = r0 + r2, i0 + i2, r0 - r2, i0 - i2
        gr, gi, hr, hi = r1 + r3, i1 + i3, r1 - r3, i1 - i3
        out[c] = (er + gr, ei + gi)
        out[c + 4] = (fr + hi, fi - hr)
        out[c + 8] = (er - gr, ei - gi)
        out[c + 12] = (fr - hi, fi + hr)
    return out


def channel_kernel(
    n, volt_ref, taps_ref, keep_ref, tcos_ref, tsin_ref, high_ref, low_ref, out_ref,
    frames, window, twist_high, twist_low, spectra, packed,
    send_a, recv_a, send_b, recv_b, own_sem,
):
    me = lax.axis_index("freq")
    spec_dev, _, channels = volt_ref.shape
    tap_count = taps_ref.shape[0]
    total = n * spec_dev
    sections = channels // AVG
    own_groups = sections // n
    pitch = spectra.shape[1] // ROWS

    barrier = pltpu.get_barrier_semaphore()
    for step in range(1, n):
        pl.semaphore_signal(
            barrier, inc=1, device_id={"freq": lax.rem(me + step, n)}, device_id_type=MESH
        )
    pl.semaphore_wait(barrier, n - 1)

    def signals_of(dev):
        return pl.ds(pl.multiple_of(dev * ROWS, ROWS), ROWS)

    copies = []
    for step in range(1, n):
        target = lax.rem(me + step, n)
        copies.append(
            pltpu.make_async_remote_copy(
                src_ref=volt_ref.at[:, signals_of(target), :],
                dst_ref=frames.at[me],
                send_sem=send_a.at[step - 1],
                recv_sem=recv_a.at[step - 1],
                device_id={"freq": target},
                device_id_type=MESH,
            )
        )
    for copy in copies:
        copy.start()
    own = pltpu.make_async_copy(volt_ref.at[:, signals_of(me), :], frames.at[me], own_sem.at[0])
    own.start()
    own.wait()
    for copy in copies:
        copy.wait()

    def filter_step(block, carry):
        lanes = pl.ds(pl.multiple_of(block * LANES, LANES), LANES)
        values = [
            frames[m // spec_dev, m % spec_dev, :, lanes].astype(jnp.float32) for m in range(total)
        ]
        taps = taps_ref[:, lanes]
        for m in range(total):
            value = taps[0:1] * values[m]
            for t in range(1, min(m + 1, tap_count)):
                value = value + taps[t : t + 1] * values[m - t]
            window[block, m * ROWS : (m + 1) * ROWS, :] = value
        return carry

    lax.fori_loop(0, channels // LANES, filter_step, 0)

    contract = (((1,), (1,)), ((), ()))
    halves = sections // LANES

    def signal_step(s, carry):
        for half in range(halves):
            pieces = [
                window[a * halves + half, pl.ds(s, total, stride=ROWS), :] for a in range(AVG)
            ]
            lanes = slice(half * LANES, (half + 1) * LANES)
            for k, (real, imag) in enumerate(short_dft(pieces)):
                co, si = tcos_ref[k : k + 1, lanes], tsin_ref[k : k + 1, lanes]
                turned = (real * co + imag * si, imag * co - real * si)
                rows = slice(k * total, (k + 1) * total)
                for part, value in enumerate(turned):
                    at = slice(part * sections + half * LANES, part * sections + (half + 1) * LANES)
                    high = value.astype(jnp.bfloat16)
                    twist_high[rows, at] = high
                    twist_low[rows, at] = (value - high.astype(jnp.float32)).astype(jnp.bfloat16)
        high = twist_high[...]
        dot = functools.partial(
            lax.dot_general, dimension_numbers=contract, preferred_element_type=jnp.float32
        )
        result = dot(high_ref[...], high) + (dot(low_ref[...], high) + dot(high_ref[...], twist_low[...]))
        at = pl.ds(pl.multiple_of(s * pitch, 8), sections)
        for part in range(AVG * total // LANES):
            spectra[part, at, :] = result[:, part * LANES : (part + 1) * LANES]
        return carry

    lax.fori_loop(0, ROWS, signal_step, 0)

    def pack_step(group, carry):
        for part in range(AVG * total // LANES):
            lanes = slice(part * LANES, (part + 1) * LANES)
            value = spectra[part, pl.ds(group, ROWS, stride=pitch), :]
            packed[group, :, lanes] = value.astype(jnp.bfloat16) * keep_ref[:, lanes]
        return carry

    lax.fori_loop(0, sections, pack_step, 0)

    def groups_of(dev):
        return pl.ds(dev * own_groups, own_groups)

    copies = []
    for step in range(1, n):
        target = lax.rem(me + step, n)
        copies.append(
            pltpu.make_async_remote_copy(
                src_ref=packed.at[groups_of(target)],
                dst_ref=out_ref.at[:, signals_of(me), :],
                send_sem=send_b.at[step - 1],
                recv_sem=recv_b.at[step - 1],
                device_id={"freq": target},
                device_id_type=MESH,
            )
        )
    for copy in copies:
        copy.start()
    own = pltpu.make_async_copy(
        packed.at[groups_of(me)], out_ref.at[:, signals_of(me), :], own_sem.at[0]
    )
    own.start()
    own.wait()
    for copy in copies:
        copy.wait()


def channelize(n, turned, filter_taps, keep):
    spec_dev, sig_dev, channels = turned.shape
    sections = channels // AVG
    total = n * spec_dev
    width = AVG * total
    pitch = sections + 8
    vmem = pl.BlockSpec(memory_space=pltpu.VMEM)
    any_space = pl.BlockSpec(memory_space=pl.ANY)
    return pl.pallas_call(
        functools.partial(channel_kernel, n),
        out_shape=jax.ShapeDtypeStruct((sections // n, sig_dev, width), jnp.bfloat16),
        in_specs=[any_space] + [vmem] * 6,
        out_specs=any_space,
        scratch_shapes=[
            pltpu.VMEM((n, spec_dev, ROWS, channels), jnp.bfloat16),
            pltpu.VMEM((channels // LANES, total * ROWS, LANES), jnp.float32),
            pltpu.VMEM((width, 2 * sections), jnp.bfloat16),
            pltpu.VMEM((width, 2 * sections), jnp.bfloat16),
            pltpu.VMEM((width // LANES, ROWS * pitch, LANES), jnp.float32),
            pltpu.VMEM((sections, ROWS, width), jnp.bfloat16),
            pltpu.SemaphoreType.DMA((n - 1,)),
            pltpu.SemaphoreType.DMA((n - 1,)),
            pltpu.SemaphoreType.DMA((n - 1,)),
            pltpu.SemaphoreType.DMA((n - 1,)),
            pltpu.SemaphoreType.DMA((1,)),
        ],
        compiler_params=pltpu.CompilerParams(
            collective_id=0, has_side_effects=True, vmem_limit_bytes=40 * 1024 * 1024
        ),
    )(turned, filter_taps, keep, *(jnp.asarray(table) for table in dft_tables(channels)))


def body(n_freq, voltages, filter_taps, station_flags):
    sig_dev, spec_dev, channels = voltages.shape
    signal_flags = jnp.repeat(station_flags, 2, axis=0).astype(jnp.float32)
    position = lax.axis_index("stn")
    own_flags = lax.dynamic_slice_in_dim(signal_flags, position * sig_dev, sig_dev, 0)
    mine = lax.dynamic_slice_in_dim(own_flags, lax.axis_index("freq") * ROWS, ROWS, 0)
    keep = jnp.tile(mine, (1, AVG)).astype(jnp.bfloat16)
    local = channelize(n_freq, voltages.transpose(1, 0, 2), filter_taps, keep)
    counts = jnp.dot(own_flags, signal_flags.T, precision=lax.Precision.HIGHEST)
    denominator = AVG * jnp.maximum(counts, 1.0)
    totals = make_tile(local, lax.all_gather(local, "stn", axis=1, tiled=True))
    return totals / denominator[None]


def solution(mesh):
    n_freq = mesh.shape["freq"]

    def whole(voltages, filter_taps, station_flags):
        signals, spectra, channels = voltages.shape
        even = signals == mesh.shape["stn"] * n_freq * ROWS
        fits = even and spectra == ROWS and channels // AVG == 2 * LANES
        inner = functools.partial(body, n_freq) if fits else plain_body
        in_specs = (P("stn", "freq", None), P(), P())
        out_specs = P("freq", "stn", None)
        mapped = jax.shard_map(
            inner, mesh=mesh, in_specs=in_specs, out_specs=out_specs, check_vma=False
        )
        return mapped(voltages, filter_taps, station_flags)

    return whole
```

```python
import functools
import math

import jax
import jax.numpy as jnp
import ml_dtypes
import numpy as np
from jax import lax
from jax.experimental import pallas as pl
from jax.experimental.pallas import tpu as pltpu
from jax.sharding import PartitionSpec as P

MESH = pl.DeviceIdType.MESH
LANES = 128
ROWS = 16
N_STN = 4
CHUNKS = 8
LAG = 3

AVG = 16


def from_behind(block, axis, distance):
    devices = range(lax.axis_size(axis))
    route = [(i - distance, i) for i in devices if i - distance in devices]
    return lax.ppermute(block, axis, route)


def dct_four(rows):
    highest = lax.Precision.HIGHEST
    count_rows, channels = rows.shape
    inner_len = 128
    outer_len = channels // inner_len
    positions = jnp.arange(channels).astype(jnp.float32)
    theta = math.pi * positions / (2 * channels)
    real_part = (rows * jnp.cos(theta)).reshape(count_rows, outer_len, inner_len)
    imag_part = (-rows * jnp.sin(theta)).reshape(count_rows, outer_len, inner_len)
    outer_idx = jnp.arange(outer_len, dtype=jnp.int32)
    outer_phase = (
        2
        * math.pi
        * (outer_idx[:, None] * outer_idx[None, :] % outer_len).astype(jnp.float32)
        / outer_len
    )
    outer_cos = jnp.cos(outer_phase)
    outer_sin = jnp.sin(outer_phase)
    section_real = jnp.einsum("pab,ak->pkb", real_part, outer_cos, precision=highest) + jnp.einsum(
        "pab,ak->pkb", imag_part, outer_sin, precision=highest
    )
    section_imag = jnp.einsum("pab,ak->pkb", imag_part, outer_cos, precision=highest) - jnp.einsum(
        "pab,ak->pkb", real_part, outer_sin, precision=highest
    )
    inner_idx = jnp.arange(inner_len, dtype=jnp.int32)
    twist_phase = (
        2 * math.pi * (outer_idx[:, None] * inner_idx[None, :]).astype(jnp.float32) / channels
    )
    twist_cos = jnp.cos(twist_phase)
    twist_sin = jnp.sin(twist_phase)
    twist_real = section_real * twist_cos + section_imag * twist_sin
    twist_imag = section_imag * twist_cos - section_real * twist_sin
    inner_phase = (
        2
        * math.pi
        * (inner_idx[:, None] * inner_idx[None, :] % inner_len).astype(jnp.float32)
        / inner_len
    )
    inner_cos = jnp.cos(inner_phase)
    inner_sin = jnp.sin(inner_phase)
    final_real = jnp.einsum("pkb,bq->pqk", twist_real, inner_cos, precision=highest) + jnp.einsum(
        "pkb,bq->pqk", twist_imag, inner_sin, precision=highest
    )
    final_imag = jnp.einsum("pkb,bq->pqk", twist_imag, inner_cos, precision=highest) - jnp.einsum(
        "pkb,bq->pqk", twist_real, inner_sin, precision=highest
    )
    final_real = final_real.reshape(count_rows, channels)
    final_imag = final_imag.reshape(count_rows, channels)
    post_angle = math.pi * (2 * positions + 1) / (4 * channels)
    return math.sqrt(2.0 / channels) * (
        final_real * jnp.cos(post_angle) + final_imag * jnp.sin(post_angle)
    )


def make_tile(mine, theirs):
    return jnp.einsum("gax,gbx->gab", mine, theirs, preferred_element_type=jnp.float32)


def plain_body(voltages, filter_taps, station_flags):
    sig_dev, spec_dev, channels = voltages.shape
    tap_count = filter_taps.shape[0]
    history_len = tap_count - 1
    reach_count = -(-history_len // spec_dev)
    earlier = []
    for distance in range(1, reach_count + 1):
        needed = min(spec_dev, history_len - (distance - 1) * spec_dev)
        earlier.append(from_behind(voltages[:, spec_dev - needed :, :], "freq", distance))
    frames = jnp.concatenate(earlier[::-1] + [voltages], axis=1)
    window = jnp.zeros((sig_dev, spec_dev, channels), jnp.float32)
    for tap_index in range(tap_count):
        offset = history_len - tap_index
        window = window + filter_taps[tap_index][None, None, :] * frames[
            :, offset : offset + spec_dev, :
        ].astype(jnp.float32)
    channelized = dct_four(window.reshape(sig_dev * spec_dev, channels)).astype(jnp.bfloat16)
    groups_all = channels // AVG
    arranged = (
        channelized.reshape(sig_dev, spec_dev, groups_all, AVG)
        .transpose(2, 0, 1, 3)
        .reshape(groups_all, sig_dev, spec_dev * AVG)
    )
    turned = lax.all_to_all(arranged, "freq", split_axis=0, concat_axis=2, tiled=True)
    signal_flags = jnp.repeat(station_flags, 2, axis=0).astype(jnp.float32)
    position = lax.axis_index("stn")
    own_flags = lax.dynamic_slice_in_dim(signal_flags, position * sig_dev, sig_dev, 0)
    keep = jnp.repeat(own_flags, AVG, axis=1).astype(jnp.bfloat16)
    local = turned * keep[None]
    counts = jnp.dot(own_flags, signal_flags.T, precision=lax.Precision.HIGHEST)
    denominator = AVG * jnp.maximum(counts, 1.0)
    totals = make_tile(local, lax.all_gather(local, "stn", axis=1, tiled=True))
    return totals / denominator[None]


def dft_tables(channels):
    sections = channels // AVG
    k_low = np.arange(AVG)[:, None]
    j_low = np.arange(sections)[None, :]
    turn = 2 * np.pi / channels * (j_low * (k_low + 0.25) + k_low / 4 + 0.125)
    scale = math.sqrt(2.0 / channels)
    twist_cos = (scale * np.cos(turn)).astype(np.float32)
    twist_sin = (scale * np.sin(turn)).astype(np.float32)
    angle = 2 * np.pi / sections * (np.arange(sections)[:, None] * (j_low + 0.25))
    full = np.concatenate([np.cos(angle), np.sin(angle)], axis=1)
    high = full.astype(ml_dtypes.bfloat16)
    low = (full - high.astype(np.float64)).astype(ml_dtypes.bfloat16)
    return twist_cos, twist_sin, high, low


def short_dft(pieces):
    quarter = {}
    for b in range(4):
        for c in range(4):
            real = pieces[b]
            imag = None
            for a in range(1, 4):
                phase = 2 * math.pi * a * (c + 0.25) / 4
                part = pieces[4 * a + b]
                real = real + part * math.cos(phase)
                term = part * -math.sin(phase)
                imag = term if imag is None else imag + term
            if b > 0:
                phase = 2 * math.pi * b * (c + 0.25) / 16
                co, si = math.cos(phase), math.sin(phase)
                real, imag = real * co + imag * si, imag * co - real * si
            quarter[b, c] = (real, imag)
    out = [None] * 16
    for c in range(4):
        (r0, i0), (r1, i1), (r2, i2), (r3, i3) = (quarter[b, c] for b in range(4))
        er, ei, fr, fi = r0 + r2, i0 + i2, r0 - r2, i0 - i2
        gr, gi, hr, hi = r1 + r3, i1 + i3, r1 - r3, i1 - i3
        out[c] = (er + gr, ei + gi)
        out[c + 4] = (fr + hi, fi - hr)
        out[c + 8] = (er - gr, ei - gi)
        out[c + 12] = (fr - hi, fi + hr)
    return out


def correlate_kernel(
    n, volt_ref, taps_ref, keep_ref, tcos_ref, tsin_ref, high_ref, low_ref, out_ref,
    frames, window, twist_high, twist_low, spectra, packed, blocks, tiles, sums,
    send_a, recv_a, send_b, recv_b, own_b, send_x, recv_x, send_t, recv_t, out_sem, own_sem,
):
    me = lax.axis_index("freq")
    spec_dev, _, channels = volt_ref.shape
    tap_count = taps_ref.shape[0]
    total = n * spec_dev
    sections = channels // AVG
    own_groups = sections // n
    pitch = spectra.shape[1] // ROWS

    barrier = pltpu.get_barrier_semaphore()
    for step in range(1, n):
        pl.semaphore_signal(
            barrier, inc=1, device_id={"freq": lax.rem(me + step, n)}, device_id_type=MESH
        )
    for step in range(1, N_STN):
        pl.semaphore_signal(
            barrier,
            inc=1,
            device_id={"stn": lax.rem(lax.axis_index("stn") + step, N_STN)},
            device_id_type=MESH,
        )
    pl.semaphore_wait(barrier, n - 1 + N_STN - 1)

    def signals_of(dev):
        return pl.ds(pl.multiple_of(dev * ROWS, ROWS), ROWS)

    copies = []
    for step in range(1, n):
        target = lax.rem(me + step, n)
        copies.append(
            pltpu.make_async_remote_copy(
                src_ref=volt_ref.at[:, signals_of(target), :],
                dst_ref=frames.at[me],
                send_sem=send_a.at[step - 1],
                recv_sem=recv_a.at[step - 1],
                device_id={"freq": target},
                device_id_type=MESH,
            )
        )
    for copy in copies:
        copy.start()
    own = pltpu.make_async_copy(volt_ref.at[:, signals_of(me), :], frames.at[me], own_sem.at[0])
    own.start()
    own.wait()
    for copy in copies:
        copy.wait()

    def filter_step(block, carry):
        lanes = pl.ds(pl.multiple_of(block * LANES, LANES), LANES)
        values = [
            frames[m // spec_dev, m % spec_dev, :, lanes].astype(jnp.float32) for m in range(total)
        ]
        taps = taps_ref[:, lanes]
        for m in range(total):
            value = taps[0:1] * values[m]
            for t in range(1, min(m + 1, tap_count)):
                value = value + taps[t : t + 1] * values[m - t]
            window[block, m * ROWS : (m + 1) * ROWS, :] = value
        return carry

    lax.fori_loop(0, channels // LANES, filter_step, 0)

    contract = (((1,), (1,)), ((), ()))
    halves = sections // LANES

    def signal_step(s, carry):
        for half in range(halves):
            pieces = [
                window[a * halves + half, pl.ds(s, total, stride=ROWS), :] for a in range(AVG)
            ]
            lanes = slice(half * LANES, (half + 1) * LANES)
            for k, (real, imag) in enumerate(short_dft(pieces)):
                co, si = tcos_ref[k : k + 1, lanes], tsin_ref[k : k + 1, lanes]
                turned = (real * co + imag * si, imag * co - real * si)
                rows = slice(k * total, (k + 1) * total)
                for part, value in enumerate(turned):
                    at = slice(part * sections + half * LANES, part * sections + (half + 1) * LANES)
                    high = value.astype(jnp.bfloat16)
                    twist_high[rows, at] = high
                    twist_low[rows, at] = (value - high.astype(jnp.float32)).astype(jnp.bfloat16)
        high = twist_high[...]
        dot = functools.partial(
            lax.dot_general, dimension_numbers=contract, preferred_element_type=jnp.float32
        )
        result = dot(high_ref[...], high) + (dot(low_ref[...], high) + dot(high_ref[...], twist_low[...]))
        at = pl.ds(pl.multiple_of(s * pitch, 8), sections)
        for part in range(AVG * total // LANES):
            spectra[part, at, :] = result[:, part * LANES : (part + 1) * LANES]
        return carry

    lax.fori_loop(0, ROWS, signal_step, 0)

    chunk = own_groups // CHUNKS
    stn = lax.axis_index("stn")

    def part_of(index):
        return pl.ds(pl.multiple_of(index * chunk, chunk), chunk)

    def turn_copy(index, step):
        target = lax.rem(me + step, n)
        return pltpu.make_async_remote_copy(
            src_ref=packed.at[pl.ds(target * own_groups + index * chunk, chunk)],
            dst_ref=blocks.at[stn, part_of(index), signals_of(me), :],
            send_sem=send_b.at[index, step - 1],
            recv_sem=recv_b.at[index, step - 1],
            device_id={"freq": target},
            device_id_type=MESH,
        )

    def own_copy(index):
        return pltpu.make_async_copy(
            packed.at[pl.ds(me * own_groups + index * chunk, chunk)],
            blocks.at[stn, part_of(index), signals_of(me), :],
            own_b.at[index],
        )

    def pack_chunk(index, carry):
        def pack_step(at, inner):
            group = (at // chunk) * own_groups + index * chunk + at % chunk
            for part in range(AVG * total // LANES):
                lanes = slice(part * LANES, (part + 1) * LANES)
                value = spectra[part, pl.ds(group, ROWS, stride=pitch), :]
                packed[group, :, lanes] = value.astype(jnp.bfloat16) * keep_ref[:, lanes]
            return inner

        lax.fori_loop(0, n * chunk, pack_step, 0)
        for step in range(1, n):
            turn_copy(index, step).start()
        own_copy(index).start()
        return carry

    lax.fori_loop(0, CHUNKS, pack_chunk, 0)

    def own_ready(index):
        for step in range(1, n):
            turn_copy(index, step).wait_recv()
        own_copy(index).wait()

    def block_copy(owner, index, send, recv, target):
        return pltpu.make_async_remote_copy(
            src_ref=blocks.at[owner, part_of(index)],
            dst_ref=blocks.at[owner, part_of(index)],
            send_sem=send_x.at[send, index],
            recv_sem=recv_x.at[recv, index],
            device_id={"stn": target},
            device_id_type=MESH,
        )

    def tile_copy(place, index, target):
        return pltpu.make_async_remote_copy(
            src_ref=tiles.at[place, part_of(index)],
            dst_ref=tiles.at[place, part_of(index)],
            send_sem=send_t.at[place, index],
            recv_sem=recv_t.at[place, index],
            device_id={"stn": target},
            device_id_type=MESH,
        )

    def out_copy(index):
        return pltpu.make_async_copy(
            sums.at[part_of(index)], out_ref.at[part_of(index)], out_sem.at[index]
        )

    def columns_of(owner):
        return pl.ds(pl.multiple_of(owner * LANES, LANES), LANES)

    def product(left, right, group):
        return lax.dot_general(
            blocks[left, group], blocks[right, group], contract, preferred_element_type=jnp.float32
        )

    def own_tile(owner, index):
        for i in range(chunk):
            group = index * chunk + i
            sums[group, :, columns_of(owner)] = product(stn, owner, group)

    def end_tile(end, owner, place, index):
        for i in range(chunk):
            group = index * chunk + i
            tiles[place, group] = product(end, owner, group).astype(jnp.bfloat16)
        tile_copy(place, index, end).start()

    last = N_STN - 1

    @pl.when((stn == 0) | (stn == last))
    def _():
        near = 1 + stn // last

        def send_step(index, carry):
            own_ready(index)
            block_copy(stn, index, 0, 0, near).start()
            own_tile(stn, index)
            return carry

        def take_step(index, carry):
            for place, owner in enumerate((near, last - near, last - stn)):
                tile_copy(place, index, near).wait_recv()
                for i in range(chunk):
                    group = index * chunk + i
                    sums[group, :, columns_of(owner)] = tiles[place, group].astype(jnp.float32)
            out_copy(index).start()
            return carry

        def drain_step(index, carry):
            block_copy(stn, index, 0, 0, near).wait_send()
            out_copy(index).wait()
            return carry

        lax.fori_loop(0, CHUNKS, send_step, 0)
        lax.fori_loop(0, CHUNKS, take_step, 0)
        lax.fori_loop(0, CHUNKS, drain_step, 0)

    @pl.when((stn > 0) & (stn < last))
    def _():
        end = (stn - 1) * last
        across = last - stn
        far = last - end

        def step_all(step, carry):
            @pl.when(step < CHUNKS)
            def _():
                own_ready(step)
                block_copy(stn, step, 0, 1, across).start()

            @pl.when((step >= 1) & (step < CHUNKS + 1))
            def _():
                index = step - 1
                block_copy(end, index, 1, 0, across).wait_recv()
                block_copy(end, index, 1, 2, across).start()
                end_tile(end, stn, 0, index)
                own_tile(stn, index)
                own_tile(end, index)

            @pl.when(step >= LAG)
            def _():
                index = step - LAG
                block_copy(across, index, 0, 1, across).wait_recv()
                end_tile(end, across, 1, index)
                own_tile(across, index)
                block_copy(far, index, 1, 2, across).wait_recv()
                end_tile(end, far, 2, index)
                own_tile(far, index)
                out_copy(index).start()

            return carry

        def drain_step(index, carry):
            block_copy(stn, index, 0, 1, across).wait_send()
            block_copy(end, index, 1, 2, across).wait_send()
            for place in range(3):
                tile_copy(place, index, end).wait_send()
            out_copy(index).wait()
            return carry

        lax.fori_loop(0, CHUNKS + LAG, step_all, 0)
        lax.fori_loop(0, CHUNKS, drain_step, 0)

    def finish_step(index, carry):
        for step in range(1, n):
            turn_copy(index, step).wait_send()
        return carry

    lax.fori_loop(0, CHUNKS, finish_step, 0)


def correlate(n, turned, filter_taps, keep):
    spec_dev, sig_dev, channels = turned.shape
    sections = channels // AVG
    total = n * spec_dev
    width = AVG * total
    groups = sections // n
    pitch = sections + 8
    vmem = pl.BlockSpec(memory_space=pltpu.VMEM)
    any_space = pl.BlockSpec(memory_space=pl.ANY)
    return pl.pallas_call(
        functools.partial(correlate_kernel, n),
        out_shape=jax.ShapeDtypeStruct((groups, sig_dev, N_STN * sig_dev), jnp.float32),
        in_specs=[any_space] + [vmem] * 6,
        out_specs=any_space,
        scratch_shapes=[
            pltpu.VMEM((n, spec_dev, ROWS, channels), jnp.bfloat16),
            pltpu.VMEM((channels // LANES, total * ROWS, LANES), jnp.float32),
            pltpu.VMEM((width, 2 * sections), jnp.bfloat16),
            pltpu.VMEM((width, 2 * sections), jnp.bfloat16),
            pltpu.VMEM((width // LANES, ROWS * pitch, LANES), jnp.float32),
            pltpu.VMEM((sections, ROWS, width), jnp.bfloat16),
            pltpu.VMEM((N_STN, groups, sig_dev, width), jnp.bfloat16),
            pltpu.VMEM((N_STN - 1, groups, sig_dev, sig_dev), jnp.bfloat16),
            pltpu.VMEM((groups, sig_dev, N_STN * sig_dev), jnp.float32),
            pltpu.SemaphoreType.DMA((n - 1,)),
            pltpu.SemaphoreType.DMA((n - 1,)),
            pltpu.SemaphoreType.DMA((CHUNKS, n - 1)),
            pltpu.SemaphoreType.DMA((CHUNKS, n - 1)),
            pltpu.SemaphoreType.DMA((CHUNKS,)),
            pltpu.SemaphoreType.DMA((2, CHUNKS)),
            pltpu.SemaphoreType.DMA((3, CHUNKS)),
            pltpu.SemaphoreType.DMA((3, CHUNKS)),
            pltpu.SemaphoreType.DMA((3, CHUNKS)),
            pltpu.SemaphoreType.DMA((CHUNKS,)),
            pltpu.SemaphoreType.DMA((1,)),
        ],
        compiler_params=pltpu.CompilerParams(
            collective_id=0, has_side_effects=True, vmem_limit_bytes=52 * 1024 * 1024
        ),
    )(turned, filter_taps, keep, *(jnp.asarray(table) for table in dft_tables(channels)))


def body(n_freq, voltages, filter_taps, station_flags):
    sig_dev, spec_dev, channels = voltages.shape
    signal_flags = jnp.repeat(station_flags, 2, axis=0).astype(jnp.float32)
    position = lax.axis_index("stn")
    own_flags = lax.dynamic_slice_in_dim(signal_flags, position * sig_dev, sig_dev, 0)
    mine = lax.dynamic_slice_in_dim(own_flags, lax.axis_index("freq") * ROWS, ROWS, 0)
    keep = jnp.tile(mine, (1, AVG)).astype(jnp.bfloat16)
    totals = correlate(n_freq, voltages.transpose(1, 0, 2), filter_taps, keep)
    counts = jnp.dot(own_flags, signal_flags.T, precision=lax.Precision.HIGHEST)
    denominator = AVG * jnp.maximum(counts, 1.0)
    return totals / denominator[None]


def solution(mesh):
    n_freq = mesh.shape["freq"]

    def whole(voltages, filter_taps, station_flags):
        signals, spectra, channels = voltages.shape
        even = signals == mesh.shape["stn"] * n_freq * ROWS
        even = even and mesh.shape["stn"] == N_STN and n_freq * ROWS == LANES
        fits = even and spectra == ROWS and channels // AVG == 2 * LANES
        inner = functools.partial(body, n_freq) if fits else plain_body
        in_specs = (P("stn", "freq", None), P(), P())
        out_specs = P("freq", "stn", None)
        mapped = jax.shard_map(
            inner, mesh=mesh, in_specs=in_specs, out_specs=out_specs, check_vma=False
        )
        return mapped(voltages, filter_taps, station_flags)

    return whole
```

```python
import functools
import math

import jax
import jax.numpy as jnp
import ml_dtypes
import numpy as np
from jax import lax
from jax.experimental import pallas as pl
from jax.experimental.pallas import tpu as pltpu
from jax.sharding import PartitionSpec as P

MESH = pl.DeviceIdType.MESH
LANES = 128
ROWS = 16
N_STN = 4
CHUNKS = 8
LAG = 3
PIECES = 4

AVG = 16


def from_behind(block, axis, distance):
    devices = range(lax.axis_size(axis))
    route = [(i - distance, i) for i in devices if i - distance in devices]
    return lax.ppermute(block, axis, route)


def dct_four(rows):
    highest = lax.Precision.HIGHEST
    count_rows, channels = rows.shape
    inner_len = 128
    outer_len = channels // inner_len
    positions = jnp.arange(channels).astype(jnp.float32)
    theta = math.pi * positions / (2 * channels)
    real_part = (rows * jnp.cos(theta)).reshape(count_rows, outer_len, inner_len)
    imag_part = (-rows * jnp.sin(theta)).reshape(count_rows, outer_len, inner_len)
    outer_idx = jnp.arange(outer_len, dtype=jnp.int32)
    outer_phase = (
        2
        * math.pi
        * (outer_idx[:, None] * outer_idx[None, :] % outer_len).astype(jnp.float32)
        / outer_len
    )
    outer_cos = jnp.cos(outer_phase)
    outer_sin = jnp.sin(outer_phase)
    section_real = jnp.einsum("pab,ak->pkb", real_part, outer_cos, precision=highest) + jnp.einsum(
        "pab,ak->pkb", imag_part, outer_sin, precision=highest
    )
    section_imag = jnp.einsum("pab,ak->pkb", imag_part, outer_cos, precision=highest) - jnp.einsum(
        "pab,ak->pkb", real_part, outer_sin, precision=highest
    )
    inner_idx = jnp.arange(inner_len, dtype=jnp.int32)
    twist_phase = (
        2 * math.pi * (outer_idx[:, None] * inner_idx[None, :]).astype(jnp.float32) / channels
    )
    twist_cos = jnp.cos(twist_phase)
    twist_sin = jnp.sin(twist_phase)
    twist_real = section_real * twist_cos + section_imag * twist_sin
    twist_imag = section_imag * twist_cos - section_real * twist_sin
    inner_phase = (
        2
        * math.pi
        * (inner_idx[:, None] * inner_idx[None, :] % inner_len).astype(jnp.float32)
        / inner_len
    )
    inner_cos = jnp.cos(inner_phase)
    inner_sin = jnp.sin(inner_phase)
    final_real = jnp.einsum("pkb,bq->pqk", twist_real, inner_cos, precision=highest) + jnp.einsum(
        "pkb,bq->pqk", twist_imag, inner_sin, precision=highest
    )
    final_imag = jnp.einsum("pkb,bq->pqk", twist_imag, inner_cos, precision=highest) - jnp.einsum(
        "pkb,bq->pqk", twist_real, inner_sin, precision=highest
    )
    final_real = final_real.reshape(count_rows, channels)
    final_imag = final_imag.reshape(count_rows, channels)
    post_angle = math.pi * (2 * positions + 1) / (4 * channels)
    return math.sqrt(2.0 / channels) * (
        final_real * jnp.cos(post_angle) + final_imag * jnp.sin(post_angle)
    )


def make_tile(mine, theirs):
    return jnp.einsum("gax,gbx->gab", mine, theirs, preferred_element_type=jnp.float32)


def plain_body(voltages, filter_taps, station_flags):
    sig_dev, spec_dev, channels = voltages.shape
    tap_count = filter_taps.shape[0]
    history_len = tap_count - 1
    reach_count = -(-history_len // spec_dev)
    earlier = []
    for distance in range(1, reach_count + 1):
        needed = min(spec_dev, history_len - (distance - 1) * spec_dev)
        earlier.append(from_behind(voltages[:, spec_dev - needed :, :], "freq", distance))
    frames = jnp.concatenate(earlier[::-1] + [voltages], axis=1)
    window = jnp.zeros((sig_dev, spec_dev, channels), jnp.float32)
    for tap_index in range(tap_count):
        offset = history_len - tap_index
        window = window + filter_taps[tap_index][None, None, :] * frames[
            :, offset : offset + spec_dev, :
        ].astype(jnp.float32)
    channelized = dct_four(window.reshape(sig_dev * spec_dev, channels)).astype(jnp.bfloat16)
    groups_all = channels // AVG
    arranged = (
        channelized.reshape(sig_dev, spec_dev, groups_all, AVG)
        .transpose(2, 0, 1, 3)
        .reshape(groups_all, sig_dev, spec_dev * AVG)
    )
    turned = lax.all_to_all(arranged, "freq", split_axis=0, concat_axis=2, tiled=True)
    signal_flags = jnp.repeat(station_flags, 2, axis=0).astype(jnp.float32)
    position = lax.axis_index("stn")
    own_flags = lax.dynamic_slice_in_dim(signal_flags, position * sig_dev, sig_dev, 0)
    keep = jnp.repeat(own_flags, AVG, axis=1).astype(jnp.bfloat16)
    local = turned * keep[None]
    counts = jnp.dot(own_flags, signal_flags.T, precision=lax.Precision.HIGHEST)
    denominator = AVG * jnp.maximum(counts, 1.0)
    totals = make_tile(local, lax.all_gather(local, "stn", axis=1, tiled=True))
    return totals / denominator[None]


def dft_tables(channels):
    sections = channels // AVG
    k_low = np.arange(AVG)[:, None]
    j_low = np.arange(sections)[None, :]
    turn = 2 * np.pi / channels * (j_low * (k_low + 0.25) + k_low / 4 + 0.125)
    scale = math.sqrt(2.0 / channels)
    twist_cos = (scale * np.cos(turn)).astype(np.float32)
    twist_sin = (scale * np.sin(turn)).astype(np.float32)
    angle = 2 * np.pi / sections * (np.arange(sections)[:, None] * (j_low + 0.25))
    full = np.concatenate([np.cos(angle), np.sin(angle)], axis=1)
    high = full.astype(ml_dtypes.bfloat16)
    low = (full - high.astype(np.float64)).astype(ml_dtypes.bfloat16)
    return twist_cos, twist_sin, high, low


def short_dft(pieces):
    quarter = {}
    for b in range(4):
        for c in range(4):
            real = pieces[b]
            imag = None
            for a in range(1, 4):
                phase = 2 * math.pi * a * (c + 0.25) / 4
                part = pieces[4 * a + b]
                real = real + part * math.cos(phase)
                term = part * -math.sin(phase)
                imag = term if imag is None else imag + term
            if b > 0:
                phase = 2 * math.pi * b * (c + 0.25) / 16
                co, si = math.cos(phase), math.sin(phase)
                real, imag = real * co + imag * si, imag * co - real * si
            quarter[b, c] = (real, imag)
    out = [None] * 16
    for c in range(4):
        (r0, i0), (r1, i1), (r2, i2), (r3, i3) = (quarter[b, c] for b in range(4))
        er, ei, fr, fi = r0 + r2, i0 + i2, r0 - r2, i0 - i2
        gr, gi, hr, hi = r1 + r3, i1 + i3, r1 - r3, i1 - i3
        out[c] = (er + gr, ei + gi)
        out[c + 4] = (fr + hi, fi - hr)
        out[c + 8] = (er - gr, ei - gi)
        out[c + 12] = (fr - hi, fi + hr)
    return out


def correlate_kernel(n, volt_ref, *refs):
    given, (out_ref, *held), rest = refs[:6], refs[6:13], refs[13:]
    (frames, window, twist_high, twist_low, spectra, packed, blocks, tiles, sums) = rest[:9]
    (send_a, recv_a, send_b, recv_b, own_b, send_x, recv_x, send_t, recv_t) = rest[9:18]
    out_sem, own_sem, given_sem = rest[18:]
    taps_ref, keep_ref, tcos_ref, tsin_ref, high_ref, low_ref = held
    loads = [
        pltpu.make_async_copy(src, dst, given_sem.at[at])
        for at, (src, dst) in enumerate(zip(given, held, strict=True))
    ]
    for load in loads:
        load.start()
    me = lax.axis_index("freq")
    spec_dev, _, channels = volt_ref.shape
    tap_count = taps_ref.shape[0]
    total = n * spec_dev
    sections = channels // AVG
    own_groups = sections // n
    pitch = spectra.shape[1] // ROWS

    barrier = pltpu.get_barrier_semaphore()
    for step in range(1, n):
        pl.semaphore_signal(
            barrier, inc=1, device_id={"freq": lax.rem(me + step, n)}, device_id_type=MESH
        )
    for step in range(1, N_STN):
        pl.semaphore_signal(
            barrier,
            inc=1,
            device_id={"stn": lax.rem(lax.axis_index("stn") + step, N_STN)},
            device_id_type=MESH,
        )
    pl.semaphore_wait(barrier, n - 1 + N_STN - 1)

    def signals_of(dev):
        return pl.ds(pl.multiple_of(dev * ROWS, ROWS), ROWS)

    piece = channels // PIECES

    def volt_copy(index, step):
        target = lax.rem(me + step, n)
        lanes = pl.ds(pl.multiple_of(index * piece, piece), piece)
        return pltpu.make_async_remote_copy(
            src_ref=volt_ref.at[:, signals_of(target), lanes],
            dst_ref=frames.at[me, :, :, lanes],
            send_sem=send_a.at[index, step - 1],
            recv_sem=recv_a.at[index, step - 1],
            device_id={"freq": target},
            device_id_type=MESH,
        )

    for index in range(PIECES):
        for step in range(1, n):
            volt_copy(index, step).start()
    own = pltpu.make_async_copy(volt_ref.at[:, signals_of(me), :], frames.at[me], own_sem.at[0])
    own.start()
    for load in loads:
        load.wait()
    own.wait()

    def filter_step(block, carry):
        lanes = pl.ds(pl.multiple_of(block * LANES, LANES), LANES)
        values = [
            frames[m // spec_dev, m % spec_dev, :, lanes].astype(jnp.float32) for m in range(total)
        ]
        taps = taps_ref[:, lanes]
        for m in range(total):
            value = taps[0:1] * values[m]
            for t in range(1, min(m + 1, tap_count)):
                value = value + taps[t : t + 1] * values[m - t]
            window[block, m * ROWS : (m + 1) * ROWS, :] = value
        return carry

    def filter_piece(index, carry):
        for step in range(1, n):
            volt_copy(index, step).wait_recv()
        blocks_in = piece // LANES
        return lax.fori_loop(index * blocks_in, (index + 1) * blocks_in, filter_step, carry)

    lax.fori_loop(0, PIECES, filter_piece, 0)

    contract = (((1,), (1,)), ((), ()))
    halves = sections // LANES

    def signal_step(s, carry):
        for half in range(halves):
            pieces = [
                window[a * halves + half, pl.ds(s, total, stride=ROWS), :] for a in range(AVG)
            ]
            lanes = slice(half * LANES, (half + 1) * LANES)
            for k, (real, imag) in enumerate(short_dft(pieces)):
                co, si = tcos_ref[k : k + 1, lanes], tsin_ref[k : k + 1, lanes]
                turned = (real * co + imag * si, imag * co - real * si)
                rows = slice(k * total, (k + 1) * total)
                for part, value in enumerate(turned):
                    at = slice(part * sections + half * LANES, part * sections + (half + 1) * LANES)
                    high = value.astype(jnp.bfloat16)
                    twist_high[rows, at] = high
                    twist_low[rows, at] = (value - high.astype(jnp.float32)).astype(jnp.bfloat16)
        high = twist_high[...]
        dot = functools.partial(
            lax.dot_general, dimension_numbers=contract, preferred_element_type=jnp.float32
        )
        result = dot(high_ref[...], high) + (dot(low_ref[...], high) + dot(high_ref[...], twist_low[...]))
        at = pl.ds(pl.multiple_of(s * pitch, 8), sections)
        for part in range(AVG * total // LANES):
            spectra[part, at, :] = result[:, part * LANES : (part + 1) * LANES]
        return carry

    lax.fori_loop(0, ROWS, signal_step, 0)

    chunk = own_groups // CHUNKS
    stn = lax.axis_index("stn")

    def part_of(index):
        return pl.ds(pl.multiple_of(index * chunk, chunk), chunk)

    def turn_copy(index, step):
        target = lax.rem(me + step, n)
        return pltpu.make_async_remote_copy(
            src_ref=packed.at[pl.ds(target * own_groups + index * chunk, chunk)],
            dst_ref=blocks.at[stn, part_of(index), signals_of(me), :],
            send_sem=send_b.at[index, step - 1],
            recv_sem=recv_b.at[index, step - 1],
            device_id={"freq": target},
            device_id_type=MESH,
        )

    def own_copy(index):
        return pltpu.make_async_copy(
            packed.at[pl.ds(me * own_groups + index * chunk, chunk)],
            blocks.at[stn, part_of(index), signals_of(me), :],
            own_b.at[index],
        )

    def pack_chunk(index, carry):
        def pack_step(at, inner):
            group = (at // chunk) * own_groups + index * chunk + at % chunk
            for part in range(AVG * total // LANES):
                lanes = slice(part * LANES, (part + 1) * LANES)
                value = spectra[part, pl.ds(group, ROWS, stride=pitch), :]
                packed[group, :, lanes] = value.astype(jnp.bfloat16) * keep_ref[:, lanes]
            return inner

        lax.fori_loop(0, n * chunk, pack_step, 0)
        for step in range(1, n):
            turn_copy(index, step).start()
        own_copy(index).start()
        return carry

    lax.fori_loop(0, CHUNKS, pack_chunk, 0)

    def own_ready(index):
        for step in range(1, n):
            turn_copy(index, step).wait_recv()
        own_copy(index).wait()

    def block_copy(owner, index, send, recv, target):
        return pltpu.make_async_remote_copy(
            src_ref=blocks.at[owner, part_of(index)],
            dst_ref=blocks.at[owner, part_of(index)],
            send_sem=send_x.at[send, index],
            recv_sem=recv_x.at[recv, index],
            device_id={"stn": target},
            device_id_type=MESH,
        )

    def tile_copy(place, index, target):
        return pltpu.make_async_remote_copy(
            src_ref=tiles.at[place, part_of(index)],
            dst_ref=tiles.at[place, part_of(index)],
            send_sem=send_t.at[place, index],
            recv_sem=recv_t.at[place, index],
            device_id={"stn": target},
            device_id_type=MESH,
        )

    def out_copy(index):
        return pltpu.make_async_copy(
            sums.at[part_of(index)], out_ref.at[part_of(index)], out_sem.at[index]
        )

    def columns_of(owner):
        return pl.ds(pl.multiple_of(owner * LANES, LANES), LANES)

    def product(left, right, group):
        return lax.dot_general(
            blocks[left, group], blocks[right, group], contract, preferred_element_type=jnp.float32
        )

    def own_tile(owner, index):
        for i in range(chunk):
            group = index * chunk + i
            sums[group, :, columns_of(owner)] = product(stn, owner, group).astype(jnp.bfloat16)

    def end_tile(end, owner, place, index):
        for i in range(chunk):
            group = index * chunk + i
            tiles[place, group] = product(end, owner, group).astype(jnp.bfloat16)
        tile_copy(place, index, end).start()

    last = N_STN - 1

    @pl.when((stn == 0) | (stn == last))
    def _():
        near = 1 + stn // last

        def send_step(index, carry):
            own_ready(index)
            block_copy(stn, index, 0, 0, near).start()
            own_tile(stn, index)
            return carry

        def take_step(index, carry):
            for place, owner in enumerate((near, last - near, last - stn)):
                tile_copy(place, index, near).wait_recv()
                for i in range(chunk):
                    group = index * chunk + i
                    sums[group, :, columns_of(owner)] = tiles[place, group]
            out_copy(index).start()
            return carry

        def drain_step(index, carry):
            block_copy(stn, index, 0, 0, near).wait_send()
            out_copy(index).wait()
            return carry

        lax.fori_loop(0, CHUNKS, send_step, 0)
        lax.fori_loop(0, CHUNKS, take_step, 0)
        lax.fori_loop(0, CHUNKS, drain_step, 0)

    @pl.when((stn > 0) & (stn < last))
    def _():
        end = (stn - 1) * last
        across = last - stn
        far = last - end

        def step_all(step, carry):
            @pl.when(step < CHUNKS)
            def _():
                own_ready(step)
                block_copy(stn, step, 0, 1, across).start()

            @pl.when((step >= 1) & (step < CHUNKS + 1))
            def _():
                index = step - 1
                block_copy(end, index, 1, 0, across).wait_recv()
                block_copy(end, index, 1, 2, across).start()
                end_tile(end, stn, 0, index)
                own_tile(stn, index)
                own_tile(end, index)

            @pl.when(step >= LAG)
            def _():
                index = step - LAG
                block_copy(across, index, 0, 1, across).wait_recv()
                end_tile(end, across, 1, index)
                own_tile(across, index)
                block_copy(far, index, 1, 2, across).wait_recv()
                end_tile(end, far, 2, index)
                own_tile(far, index)
                out_copy(index).start()

            return carry

        def drain_step(index, carry):
            block_copy(stn, index, 0, 1, across).wait_send()
            block_copy(end, index, 1, 2, across).wait_send()
            for place in range(3):
                tile_copy(place, index, end).wait_send()
            out_copy(index).wait()
            return carry

        lax.fori_loop(0, CHUNKS + LAG, step_all, 0)
        lax.fori_loop(0, CHUNKS, drain_step, 0)

    for index in range(PIECES):
        for step in range(1, n):
            volt_copy(index, step).wait_send()

    def finish_step(index, carry):
        for step in range(1, n):
            turn_copy(index, step).wait_send()
        return carry

    lax.fori_loop(0, CHUNKS, finish_step, 0)


def correlate(n, turned, filter_taps, keep):
    spec_dev, sig_dev, channels = turned.shape
    sections = channels // AVG
    total = n * spec_dev
    width = AVG * total
    groups = sections // n
    pitch = sections + 8
    any_space = pl.BlockSpec(memory_space=pl.ANY)
    tables = (filter_taps, keep, *(jnp.asarray(table) for table in dft_tables(channels)))
    return pl.pallas_call(
        functools.partial(correlate_kernel, n),
        out_shape=jax.ShapeDtypeStruct((groups, sig_dev, N_STN * sig_dev), jnp.bfloat16),
        in_specs=[any_space] * 7,
        out_specs=any_space,
        scratch_shapes=[pltpu.VMEM(table.shape, table.dtype) for table in tables]
        + [
            pltpu.VMEM((n, spec_dev, ROWS, channels), jnp.bfloat16),
            pltpu.VMEM((channels // LANES, total * ROWS, LANES), jnp.float32),
            pltpu.VMEM((width, 2 * sections), jnp.bfloat16),
            pltpu.VMEM((width, 2 * sections), jnp.bfloat16),
            pltpu.VMEM((width // LANES, ROWS * pitch, LANES), jnp.float32),
            pltpu.VMEM((sections, ROWS, width), jnp.bfloat16),
            pltpu.VMEM((N_STN, groups, sig_dev, width), jnp.bfloat16),
            pltpu.VMEM((N_STN - 1, groups, sig_dev, sig_dev), jnp.bfloat16),
            pltpu.VMEM((groups, sig_dev, N_STN * sig_dev), jnp.bfloat16),
            pltpu.SemaphoreType.DMA((PIECES, n - 1)),
            pltpu.SemaphoreType.DMA((PIECES, n - 1)),
            pltpu.SemaphoreType.DMA((CHUNKS, n - 1)),
            pltpu.SemaphoreType.DMA((CHUNKS, n - 1)),
            pltpu.SemaphoreType.DMA((CHUNKS,)),
            pltpu.SemaphoreType.DMA((2, CHUNKS)),
            pltpu.SemaphoreType.DMA((3, CHUNKS)),
            pltpu.SemaphoreType.DMA((3, CHUNKS)),
            pltpu.SemaphoreType.DMA((3, CHUNKS)),
            pltpu.SemaphoreType.DMA((CHUNKS,)),
            pltpu.SemaphoreType.DMA((1,)),
            pltpu.SemaphoreType.DMA((6,)),
        ],
        compiler_params=pltpu.CompilerParams(
            collective_id=0, has_side_effects=True, vmem_limit_bytes=52 * 1024 * 1024
        ),
    )(turned, *tables)


def body(n_freq, voltages, filter_taps, station_flags):
    sig_dev, spec_dev, channels = voltages.shape
    signal_flags = jnp.repeat(station_flags, 2, axis=0).astype(jnp.float32)
    position = lax.axis_index("stn")
    own_flags = lax.dynamic_slice_in_dim(signal_flags, position * sig_dev, sig_dev, 0)
    mine = lax.dynamic_slice_in_dim(own_flags, lax.axis_index("freq") * ROWS, ROWS, 0)
    keep = jnp.tile(mine, (1, AVG)).astype(jnp.bfloat16)
    totals = correlate(n_freq, voltages.transpose(1, 0, 2), filter_taps, keep)
    counts = jnp.dot(own_flags, signal_flags.T, precision=lax.Precision.HIGHEST)
    denominator = AVG * jnp.maximum(counts, 1.0)
    return totals.astype(jnp.float32) / denominator[None]


def solution(mesh):
    n_freq = mesh.shape["freq"]

    def whole(voltages, filter_taps, station_flags):
        signals, spectra, channels = voltages.shape
        even = signals == mesh.shape["stn"] * n_freq * ROWS
        even = even and mesh.shape["stn"] == N_STN and n_freq * ROWS == LANES
        fits = even and spectra == ROWS and channels // AVG == 2 * LANES
        inner = functools.partial(body, n_freq) if fits else plain_body
        in_specs = (P("stn", "freq", None), P(), P())
        out_specs = P("freq", "stn", None)
        mapped = jax.shard_map(
            inner, mesh=mesh, in_specs=in_specs, out_specs=out_specs, check_vma=False
        )
        return mapped(voltages, filter_taps, station_flags)

    return whole
```
